128 devices in a mesh: inp: 32 (over x, y_lo, z), grp: 4 (over y_hi, core).
Axes of the slice: x: 4, y: 4 (y_hi: 2, y_lo: 2; y = y_hi * 2 + y_lo), z: 4, core: 2. Of those that a mesh axis runs over, the one named last changes fastest.
Arguments:
- raw: bfloat16 [4096, 268288], P(('inp', 'grp')), may hold values from -6 to 6
- steer: int32 [256, 4096], P(None, ('inp', 'grp')), may hold values from 0 to 255
- slot_map: int32 [4096], replicated, may hold values from 0 to 4095, each once
Outputs:
- visibility: float32 [2, 32768, 4096], P(None, ('inp', 'grp'))
- beam_power: float32 [512, 256], P(('inp', 'grp'))
The draws below stay inside these ranges and needn't reach their ends.
Inputs may be any that keep to these rules, and one draw needn't show every extreme that they name: slot_map is a permutation of the 4096 streams. steer's values matter only modulo 256; a program may carry them between devices in any exact form, several to a word.
All inputs are finite; a program needn't handle non-finite values.
Results may differ from the reference program's by a relative error of at most 0.0069.
Values may be sent and summed in bfloat16 or wider, within the bound.
A program may use at most 128 MiB of HBM per device.

```python
import math
import jax
import jax.numpy as jnp
from jax import lax

NS = 4096
NFFT = 2048
BEAMS = 256
TAPS = 4
PHASES = 256
CH_GRP = 128
ROWS = 64
FRAMES = 128
SAMPLES = 268288
N_INP = 32
N_GRP = 4


def place_ends(entries, rng, low, high):
    longest = entries.shape.index(max(entries.shape))
    spots = []
    for shift in (0, 1):
        where = [jax.random.randint(jax.random.fold_in(rng, axis), (), 0, length) for axis, length in enumerate(entries.shape)]
        where[longest] = (where[longest] + shift) % entries.shape[longest]
        spots.append(tuple(where))
    return entries.at[spots[0]].set(low).at[spots[1]].set(high)


def steps_of(rng, shape, cuts, low, largest):
    def one(dim, blocks):
        draws = jax.random.uniform(jax.random.fold_in(jax.random.fold_in(rng, 6), dim), (blocks,), jnp.float32, low / len(cuts), largest / len(cuts))
        return jnp.repeat(jnp.exp(draws), shape[dim] // blocks).reshape((-1,) + (1,) * (len(shape) - dim - 1))

    factor_of = one(*cuts[0])
    for cut in cuts[1:]:
        factor_of = factor_of * one(*cut)
    return factor_of


def centred(stream_key, dims, scale, most, cuts=(), kind=jnp.bfloat16):
    values = jax.random.normal(stream_key, dims, jnp.float32) * scale
    if len(cuts) > 0:
        values = steps_of(stream_key, dims, cuts, -0.22, 0.18) * values
    return jnp.clip(values, min=-most, max=most).astype(kind)


def setup_inputs(seed: int = 0) -> dict:
    key_list = jax.random.split(jax.random.key(seed), 4)
    return {
        "raw": centred(key_list[0], (NS, SAMPLES), 1.0, 6.0, ((0, 128),)),
        "steer": place_ends(jax.random.randint(key_list[1], (BEAMS, NS), 0, PHASES), jax.random.fold_in(key_list[1], 1), 0, PHASES - 1).astype(jnp.int32),
        "slot_map": jax.random.permutation(key_list[2], NS).astype(jnp.int32),
    }


def prototype():
    pos = jnp.arange(TAPS * NFFT, dtype=jnp.float32) + 0.5
    arg = pos / NFFT - TAPS / 2.0
    window = 0.5 - 0.5 * jnp.cos(2.0 * math.pi * pos / (TAPS * NFFT))
    return (jnp.sinc(arg) * window).reshape(TAPS, NFFT)

def channel_numbers():
    sub = NFFT // 2 // N_GRP
    ch_dev = CH_GRP // N_INP
    order = jnp.arange(CH_GRP * N_GRP, dtype=jnp.int32)
    device = order // ch_dev
    inner = order % ch_dev
    return (device % N_GRP * sub + (sub - CH_GRP) // 2 + device // N_GRP * ch_dev + inner).astype(jnp.int32)

def dft_table(chans):
    sample = jnp.arange(NFFT, dtype=jnp.int32)
    phase = (chans[:, None] * sample[None, :] % NFFT).astype(jnp.float32)
    angle = 2.0 * math.pi * phase / NFFT
    scale = 1.0 / math.sqrt(NFFT)
    return jnp.stack([jnp.cos(angle) * scale, -jnp.sin(angle) * scale]).astype(jnp.bfloat16)

def reference(raw, steer, slot_map):
    proto = prototype()
    chans = channel_numbers()
    table = dft_table(chans).astype(jnp.float32)
    block = math.gcd(NS, 256)
    ch_win = CH_GRP * N_GRP

    def spec_block(rows):
        view = rows.reshape(block, FRAMES + TAPS - 1, NFFT).astype(jnp.float32)
        total = jnp.zeros((block, FRAMES, NFFT), jnp.float32)
        for tap in range(TAPS):
            total = total + proto[tap][None, None, :] * view[:, tap:tap + FRAMES, :]
        filtered = total.astype(jnp.bfloat16).astype(jnp.float32)
        return jnp.einsum('rcn,sfn->crsf', table, filtered).astype(jnp.bfloat16)
    pieces = lax.map(spec_block, raw.reshape(NS // block, block, SAMPLES))
    spectra = pieces.transpose(1, 2, 0, 3, 4).reshape(ch_win, 2, NS, FRAMES)

    def per_chan(pair):
        chan, number = pair
        permuted = jnp.take(chan, slot_map, axis=1)
        left = permuted[:, :ROWS].reshape(2 * ROWS, FRAMES)
        right = permuted.reshape(2 * NS, FRAMES)
        prod = jnp.dot(left, right.T, preferred_element_type=jnp.float32)
        real_part = (prod[:ROWS, :NS] + prod[ROWS:, NS:]) / FRAMES
        imag_part = (prod[:ROWS, NS:] - prod[ROWS:, :NS]) / FRAMES
        phase = (steer * number % PHASES).astype(jnp.float32)
        angle = 2.0 * math.pi * phase / PHASES
        wcos = (jnp.cos(angle) / math.sqrt(NS)).astype(jnp.bfloat16)
        wsin = (jnp.sin(angle) / math.sqrt(NS)).astype(jnp.bfloat16)
        real_in, imag_in = (chan[0], chan[1])
        beam_re = jnp.dot(wcos, real_in, preferred_element_type=jnp.float32) + jnp.dot(wsin, imag_in, preferred_element_type=jnp.float32)
        beam_im = jnp.dot(wcos, imag_in, preferred_element_type=jnp.float32) - jnp.dot(wsin, real_in, preferred_element_type=jnp.float32)
        power = lax.optimization_barrier(jnp.sum(beam_re * beam_re + beam_im * beam_im, axis=1)) / FRAMES
        return (jnp.stack([real_part, imag_part]), power)
    tiles, power = lax.map(per_chan, (spectra, chans))
    visibility = tiles.transpose(1, 0, 2, 3).reshape(2, ch_win * ROWS, NS)
    return (visibility, power)
```

```python
import functools
import math

import jax
import jax.numpy as jnp
import numpy as np
from jax import lax
from jax.experimental import pallas as pl
from jax.experimental.pallas import tpu as pltpu
from jax.sharding import PartitionSpec as P

MESH = pl.DeviceIdType.MESH
NS = 4096
NFFT = 2048
BEAMS = 256
TAPS = 4
CH_GRP = 128
ROWS = 64
FRAMES = 128
N_INP = 32
N_GRP = 4
COUNT = N_INP * N_GRP
CH_DEV = CH_GRP * N_GRP // COUNT
NS_DEV = NS // COUNT
SAMPLES = (FRAMES + TAPS - 1) * NFFT
HALVES = 2
NS_HALF = NS_DEV // HALVES
PARTS = 2 * CH_DEV
BLOCK = NS_HALF * PARTS
MIB = 2**20
F32 = jnp.float32
BF16 = jnp.bfloat16


def prototype():
    pos = np.arange(TAPS * NFFT, dtype=np.float64) + 0.5
    arg = pos / NFFT - TAPS / 2.0
    window = 0.5 - 0.5 * np.cos(2.0 * math.pi * pos / (TAPS * NFFT))
    return (np.sinc(arg) * window).reshape(TAPS, NFFT).astype(np.float32)


def dft_table():
    sub = NFFT // 2 // N_GRP
    order = np.arange(CH_GRP * N_GRP)
    device, inner = order // CH_DEV, order % CH_DEV
    chans = device % N_GRP * sub + (sub - CH_GRP) // 2 + device // N_GRP * CH_DEV + inner
    angle = 2.0 * math.pi * (chans[:, None] * np.arange(NFFT)[None, :] % NFFT) / NFFT
    both = np.stack([np.cos(angle), -np.sin(angle)], axis=1) / math.sqrt(NFFT)
    return both.astype(np.float32).astype(jnp.bfloat16).reshape(COUNT * PARTS, NFFT)


def orbits():
    seen, out = set(), []
    for a in range(4):
        for b in range(4):
            for c in range(4):
                if (a, b, c) == (0, 0, 0) or (a, b, c) in seen:
                    continue
                orbit = []
                for turn in ((a, b, c), (b, c, a), (c, a, b)):
                    for sign in (1, -1):
                        item = tuple(sign * v % 4 for v in turn)
                        if item not in orbit:
                            orbit.append(item)
                seen.update(orbit)
                out.append(orbit)
    return out


def neighbour(dx, dy, dz, dc):
    inp, grp = lax.axis_index("inp"), lax.axis_index("grp")
    x = (inp // 8 + dx) % 4
    y = (grp // 2 * 2 + inp // 4 % 2 + dy) % 4
    z = (inp % 4 + dz) % 4
    core = (grp % 2 + dc) % 2
    return x * 8 + y % 2 * 4 + z, y // 2 * 2 + core


def for_peers(body):
    for orbit in orbits():
        a, b, c = orbit[0]
        size = len(orbit)
        pairs = 2 if size in (6, 2) else 1

        def step(i, carry, a=a, b=b, c=c, size=size, pairs=pairs):
            core, item = i // size, i % size
            turn, sign = item // pairs, 1 - 2 * (item % pairs)
            dx = jnp.where(turn == 0, a, jnp.where(turn == 1, b, c))
            dy = jnp.where(turn == 0, b, jnp.where(turn == 1, c, a))
            dz = jnp.where(turn == 0, c, jnp.where(turn == 1, a, b))
            body(*neighbour(dx * sign + 4, dy * sign + 4, dz * sign + 4, core))
            return carry

        lax.fori_loop(0, 2 * size, step, 0)
    body(*neighbour(0, 0, 0, 1))


def sine(m):
    u = m.astype(F32) * (1.0 / 64.0)
    v = u * u
    p = 1.5148419e-4 * v - 4.673767e-3
    p = p * v + 7.968967e-2
    p = p * v - 6.4596371e-1
    p = p * v + 1.5707963
    return p * u * (1.0 / math.sqrt(NS))


def weights(phase):
    wcos = sine(jnp.abs((phase & 255) - 128) - 64)
    wsin = sine(jnp.abs(((phase - 64) & 255) - 128) - 64)
    return wcos.astype(BF16), wsin.astype(BF16)


def channel_kernel(
    raw, table, proto, steer, x_ref, power,
    rawb, tab, fb, turn, send, xb, xf, beam, wts, words, packs, pack,
    raw_sem, tab_sem, send_sem, recv_sem, own_sem, x_sem, st_send, st_recv,
):
    inp, grp = lax.axis_index("inp"), lax.axis_index("grp")
    me = inp * N_GRP + grp

    for_peers(lambda i, g: pl.semaphore_signal(
        pltpu.get_barrier_semaphore(), inc=1, device_id=(i, g), device_id_type=MESH))

    cuts = (0, 35, 67, 99, 131)

    def raw_copy(half, part):
        lo, hi = cuts[part] * NFFT, cuts[part + 1] * NFFT
        return pltpu.make_async_copy(
            raw.at[pl.ds(half * NS_HALF, NS_HALF), pl.ds(lo, hi - lo)],
            rawb.at[:, pl.ds(lo, hi - lo)], raw_sem.at[part])

    for part in range(4):
        raw_copy(0, part).start()
    tab_copy = pltpu.make_async_copy(table, tab, tab_sem)
    tab_copy.start()

    word = steer[0:64, :] & 255
    for byte in range(1, 4):
        word = word + (steer[byte * 64:(byte + 1) * 64, :] & 255) * (1 << (8 * byte))
    words[...] = jnp.zeros_like(words)
    words[:, 0:NS_DEV] = word
    lane = lax.broadcasted_iota(jnp.int32, (8, 128), 1) // 16
    for half in range(HALVES):
        total = jnp.zeros((8, 128), jnp.int32)
        for eq in range(8):
            moved = pltpu.roll(words[eq * 8:(eq + 1) * 8, :], (eq - half) * 16 % 128, 1)
            total = jnp.where(lane == eq, moved, total)
        packs[me, pl.ds(half * 8, 8), :] = total

    def filter_part(part):
        def body(it, carry):
            f0 = part * 32 + it // 8 * 16
            for sub in range(2):
                n0 = pl.multiple_of(it % 8 * 256 + sub * 128, 128)
                vals = [
                    rawb[:, pl.ds(pl.multiple_of((f0 + g) * NFFT + n0, 128), 128)].astype(F32)
                    for g in range(16 + TAPS - 1)
                ]
                taps = [proto[t:t + 1, pl.ds(n0, 128)] for t in range(TAPS)]
                for f in range(16):
                    acc = taps[0] * vals[f]
                    for t in range(1, TAPS):
                        acc = acc + taps[t] * vals[f + t]
                    turn[sub, f * NS_HALF:(f + 1) * NS_HALF, :] = acc
                for s in range(NS_HALF):
                    rows = turn[sub, pl.ds(s, 16, stride=NS_HALF), :].astype(BF16)
                    fb[pl.ds(pl.multiple_of(s * FRAMES + f0, 16), 16), pl.ds(n0, 128)] = rows
            return carry

        lax.fori_loop(0, 16, body, 0)

    def transform(half):
        def body(pair, carry):
            cols = fb[pl.ds(pl.multiple_of(pair * 256, 256), 256), :]
            for kt in range(4):
                out = lax.dot_general(
                    tab[kt * 256:(kt + 1) * 256, :], cols,
                    (((1,), (1,)), ((), ())), preferred_element_type=F32)
                first = out[:, :128].reshape(32, PARTS, 128)
                second = out[:, 128:].reshape(32, PARTS, 128)
                both = jnp.concatenate([first, second], axis=1).astype(BF16)
                send[half, kt * 32:(kt + 1) * 32, pl.ds(pl.multiple_of(pair * 16, 16), 16), :] = both
            return carry

        lax.fori_loop(0, NS_HALF // 2, body, 0)

    def spread(half):
        def one(i, g):
            pltpu.make_async_remote_copy(
                src_ref=send.at[half, i * N_GRP + g],
                dst_ref=x_ref.at[me, pl.ds(half * BLOCK, BLOCK)],
                send_sem=send_sem.at[half], recv_sem=recv_sem.at[half],
                device_id=(i, g), device_id_type=MESH).start()

        for_peers(one)
        pltpu.make_async_copy(
            send.at[half, me], x_ref.at[me, pl.ds(half * BLOCK, BLOCK)], own_sem.at[half]).start()

    def steer_copies(stage):
        if stage == 0:
            src = packs.at[pl.ds(me, 1)]
            to = [(inp, (grp + k) % 4) for k in range(1, 4)]
        elif stage == 1:
            src = packs.at[pl.ds(inp * 4, 4)]
            to = [(inp // 4 * 4 + (inp + k) % 4, grp) for k in range(1, 4)]
        else:
            src = packs.at[pl.ds(inp // 4 * 16, 16)]
            to = [((inp // 4 + k) % 8 * 4 + inp % 4, grp) for k in range(1, 8)]
        return [
            pltpu.make_async_remote_copy(
                src_ref=src, dst_ref=src, send_sem=st_send.at[stage], recv_sem=st_recv.at[stage],
                device_id=d, device_id_type=MESH) for d in to
        ]

    def steer_start(stage):
        for copy in steer_copies(stage):
            copy.start()

    def steer_wait(stage):
        size = (3, 12, 112)[stage]
        done = pltpu.make_async_remote_copy(
            src_ref=packs.at[pl.ds(0, size)], dst_ref=packs.at[pl.ds(0, size)],
            send_sem=st_send.at[stage], recv_sem=st_recv.at[stage],
            device_id=(inp, (grp + 1) % 4), device_id_type=MESH)
        done.wait_send()
        done.wait_recv()

    for part in range(4):
        raw_copy(0, part).wait()
        filter_part(part)
    for part in range(4):
        raw_copy(1, part).start()
    pl.semaphore_wait(pltpu.get_barrier_semaphore(), COUNT - 1)
    steer_start(0)
    tab_copy.wait()
    transform(0)
    spread(0)
    steer_wait(0)
    steer_start(1)
    for part in range(4):
        raw_copy(1, part).wait()
        filter_part(part)
    steer_wait(1)
    steer_start(2)
    transform(1)
    spread(1)
    steer_wait(2)

    def weigh(it, carry):
        half, tile = it // 16, it % 16
        base = tile * 8
        for eq in range(8):
            total = jnp.zeros((8, 128), jnp.int32)
            for dd in range(8):
                block = packs[base + dd, pl.ds(pl.multiple_of(half * 8, 8), 8), :]
                total = jnp.where(lane == dd, pltpu.roll(block, (dd - eq) * 16 % 128, 1), total)
            pack[eq * 8:(eq + 1) * 8, :] = total
        col = pl.multiple_of(tile * 128, 128)
        for byte in range(4):
            index = (pack[...] >> (8 * byte)) & 255
            for j in range(CH_DEV):
                wcos, wsin = weights(index * (inp * CH_DEV + ((NFFT // 2 // N_GRP - CH_GRP) // 2 + j)))
                wts[j, half, byte * 64:(byte + 1) * 64, pl.ds(col, 128)] = wcos
                wts[j, half, byte * 64:(byte + 1) * 64, pl.ds(col + 2048, 128)] = wsin
        return carry

    lax.fori_loop(0, 16 * HALVES, weigh, 0)
    beam[...] = jnp.zeros_like(beam)

    for half in range(HALVES):
        done = pltpu.make_async_remote_copy(
            src_ref=send.at[half, pl.ds(0, COUNT - 1)],
            dst_ref=x_ref.at[pl.ds(0, COUNT - 1), pl.ds(half * BLOCK, BLOCK)],
            send_sem=send_sem.at[half], recv_sem=recv_sem.at[half],
            device_id=(inp, (grp + 1) % 4), device_id_type=MESH)
        done.wait_send()
        done.wait_recv()
        pltpu.make_async_copy(
            send.at[half, me], x_ref.at[me, pl.ds(half * BLOCK, BLOCK)], own_sem.at[half]).wait()
        fetch = pltpu.make_async_copy(x_ref.at[:, pl.ds(half * BLOCK, BLOCK)], xb, x_sem)
        fetch.start()
        fetch.wait()

        def add(sb, carry, half=half):
            xf[...] = xb[pl.ds(sb * 16, 16)].astype(F32).reshape(16 * BLOCK, 128)
            for j in range(CH_DEV):
                re = xf[pl.ds(2 * j, 256, stride=PARTS), :]
                im = xf[pl.ds(2 * j + 1, 256, stride=PARTS), :]
                ab = jnp.concatenate([re, im], axis=1).astype(BF16)
                ba = jnp.concatenate([im, -re], axis=1).astype(BF16)
                col = pl.multiple_of(sb * 256, 256)
                beam[j] += jnp.dot(
                    wts[j, half, :, pl.ds(col, 256)], ab, preferred_element_type=F32
                ) + jnp.dot(
                    wts[j, half, :, pl.ds(col + 2048, 256)], ba, preferred_element_type=F32)
            return carry

        lax.fori_loop(0, 8, add, 0)

    for j in range(CH_DEV):
        value = beam[j]
        square = value * value
        folded = (square[:, :128] + square[:, 128:]).T
        power[j:j + 1, :] = jnp.sum(folded, axis=0, keepdims=True) * (1.0 / FRAMES)


def gram_kernel(slots, x_ref, out, xb, xf, yf, left, sems):
    step = pl.program_id(0)

    def gather(first, count):
        def body(i, carry):
            for k in range(8):
                q = i * 8 + k
                row = pl.multiple_of(slots[first + q] * PARTS, PARTS)
                yf[pl.ds(pl.multiple_of(q * PARTS, PARTS), PARTS), :] = xf[pl.ds(row, PARTS), :]
            return carry

        lax.fori_loop(0, count // 8, body, 0)

    @pl.when(step == 0)
    def _():
        copies = [
            pltpu.make_async_copy(
                x_ref.at[pl.ds(k * 16, 16)], xb.at[pl.ds(k * 16, 16)], sems.at[k]) for k in range(8)
        ]
        for copy in copies:
            copy.start()
        for k, copy in enumerate(copies):
            copy.wait()

            def widen(i, carry):
                dev = k * 16 + i
                rows = pl.ds(pl.multiple_of(dev * 256, 256), 256)
                xf[rows, :] = xb[dev].astype(F32)
                return carry

            lax.fori_loop(0, 16, widen, 0)
        gather(0, ROWS)
        for j in range(CH_DEV):
            re = yf[pl.ds(2 * j, ROWS, stride=PARTS), :]
            im = yf[pl.ds(2 * j + 1, ROWS, stride=PARTS), :]
            upper = jnp.concatenate([re, im], axis=1)
            lower = jnp.concatenate([-im, re], axis=1)
            left[j] = jnp.concatenate([upper, lower], axis=0).astype(BF16)

    gather(step * 256, 256)
    for j in range(CH_DEV):
        re = yf[pl.ds(2 * j, 256, stride=PARTS), :]
        im = yf[pl.ds(2 * j + 1, 256, stride=PARTS), :]
        right = jnp.concatenate([re, im], axis=1).astype(BF16)
        prod = lax.dot_general(
            left[j], right, (((1,), (1,)), ((), ())), preferred_element_type=F32)
        prod = prod * (1.0 / FRAMES)
        out[0, j * ROWS:(j + 1) * ROWS, :] = prod[:ROWS]
        out[1, j * ROWS:(j + 1) * ROWS, :] = prod[ROWS:]


def per_device(raw, steer, slot_map):
    anywhere = pl.BlockSpec(memory_space=pl.ANY)
    vmem = pl.BlockSpec(memory_space=pltpu.VMEM)
    dma = pltpu.SemaphoreType.DMA
    spectra, power = pl.pallas_call(
        channel_kernel,
        out_shape=(
            jax.ShapeDtypeStruct((COUNT, HALVES * BLOCK, FRAMES), BF16),
            jax.ShapeDtypeStruct((CH_DEV, BEAMS), F32),
        ),
        in_specs=[anywhere, anywhere, vmem, vmem],
        out_specs=(anywhere, vmem),
        scratch_shapes=[
            pltpu.VMEM((NS_HALF, SAMPLES), BF16),
            pltpu.VMEM((COUNT * PARTS, NFFT), BF16),
            pltpu.VMEM((NS_HALF * FRAMES, NFFT), BF16),
            pltpu.VMEM((2, 16 * NS_HALF, 128), F32),
            pltpu.VMEM((HALVES, COUNT, BLOCK, FRAMES), BF16),
            pltpu.VMEM((COUNT, BLOCK, FRAMES), BF16),
            pltpu.VMEM((16 * BLOCK, FRAMES), F32),
            pltpu.VMEM((CH_DEV, BEAMS, 2 * FRAMES), F32),
            pltpu.VMEM((CH_DEV, HALVES, BEAMS, NS), BF16),
            pltpu.VMEM((64, 128), jnp.int32),
            pltpu.VMEM((COUNT, 16, 128), jnp.int32),
            pltpu.VMEM((64, 128), jnp.int32),
            dma((4,)), dma, dma((HALVES,)), dma((HALVES,)), dma((HALVES,)), dma,
            dma((3,)), dma((3,)),
        ],
        compiler_params=pltpu.CompilerParams(
            collective_id=0, has_side_effects=True, vmem_limit_bytes=62 * MIB),
        name="channelize",
    )(raw, jnp.asarray(dft_table()), jnp.asarray(prototype()), steer)
    visibility = pl.pallas_call(
        gram_kernel,
        out_shape=jax.ShapeDtypeStruct((2, CH_DEV * ROWS, NS), F32),
        grid=(NS // 256,),
        in_specs=[pl.BlockSpec(memory_space=pltpu.SMEM), anywhere],
        out_specs=pl.BlockSpec((2, CH_DEV * ROWS, 256), lambda i: (0, 0, i)),
        scratch_shapes=[
            pltpu.VMEM((COUNT, HALVES * BLOCK, FRAMES), BF16),
            pltpu.VMEM((NS * PARTS, FRAMES), F32),
            pltpu.VMEM((256 * PARTS, FRAMES), F32),
            pltpu.VMEM((CH_DEV, 2 * ROWS, 2 * FRAMES), BF16),
            dma((8,)),
        ],
        compiler_params=pltpu.CompilerParams(vmem_limit_bytes=48 * MIB),
        name="gram",
    )(slot_map, spectra)
    return visibility, power


def solution(mesh):
    in_specs = (P(("inp", "grp"), None), P(None, ("inp", "grp")), P())
    out_specs = (P(None, ("inp", "grp"), None), P(("inp", "grp"), None))
    return jax.shard_map(
        per_device, mesh=mesh, in_specs=in_specs, out_specs=out_specs, check_vma=False
    )
```

```python
import functools
import math

import jax
import jax.numpy as jnp
import numpy as np
from jax import lax
from jax.experimental import pallas as pl
from jax.experimental.pallas import tpu as pltpu
from jax.sharding import PartitionSpec as P

MESH = pl.DeviceIdType.MESH
NS = 4096
NFFT = 2048
BEAMS = 256
TAPS = 4
CH_GRP = 128
ROWS = 64
FRAMES = 128
N_INP = 32
N_GRP = 4
COUNT = N_INP * N_GRP
CH_DEV = CH_GRP * N_GRP // COUNT
NS_DEV = NS // COUNT
SAMPLES = (FRAMES + TAPS - 1) * NFFT
CHUNKS = 4
NS_CHUNK = NS_DEV // CHUNKS
PARTS = 2 * CH_DEV
BLOCK = NS_CHUNK * PARTS
KEYS = COUNT * NS_CHUNK
MIB = 2**20
F32 = jnp.float32
BF16 = jnp.bfloat16


def prototype():
    pos = np.arange(TAPS * NFFT, dtype=np.float64) + 0.5
    arg = pos / NFFT - TAPS / 2.0
    window = 0.5 - 0.5 * np.cos(2.0 * math.pi * pos / (TAPS * NFFT))
    return (np.sinc(arg) * window).reshape(TAPS, NFFT).astype(np.float32)


def dft_table():
    sub = NFFT // 2 // N_GRP
    order = np.arange(CH_GRP * N_GRP)
    device, inner = order // CH_DEV, order % CH_DEV
    chans = device % N_GRP * sub + (sub - CH_GRP) // 2 + device // N_GRP * CH_DEV + inner
    angle = 2.0 * math.pi * (chans[:, None] * np.arange(NFFT)[None, :] % NFFT) / NFFT
    both = np.stack([np.cos(angle), -np.sin(angle)], axis=1) / math.sqrt(NFFT)
    return both.astype(np.float32).astype(jnp.bfloat16).reshape(COUNT * PARTS, NFFT)


def orbits():
    seen, out = set(), []
    for a in range(4):
        for b in range(4):
            for c in range(4):
                if (a, b, c) == (0, 0, 0) or (a, b, c) in seen:
                    continue
                orbit = []
                for sign in (1, -1):
                    for turn in ((a, b, c), (b, c, a), (c, a, b)):
                        item = tuple(sign * v % 4 for v in turn)
                        if item not in orbit:
                            orbit.append(item)
                seen.update(orbit)
                out.append(orbit)
    return out


def neighbour(dx, dy, dz, dc):
    inp, grp = lax.axis_index("inp"), lax.axis_index("grp")
    x = (inp // 8 + dx) % 4
    y = (grp // 2 * 2 + inp // 4 % 2 + dy) % 4
    z = (inp % 4 + dz) % 4
    core = (grp % 2 + dc) % 2
    return x * 8 + y % 2 * 4 + z, y // 2 * 2 + core


def for_peers(body):
    way = 1 - 2 * (lax.axis_index("grp") % 2)
    for orbit in orbits():
        a, b, c = orbit[0]
        size = len(orbit)
        turns = 3 if size % 3 == 0 else 1

        def step(i, carry, a=a, b=b, c=c, size=size, turns=turns):
            core, item = i // size, i % size
            turn, sign = item % turns, (1 - 2 * (item // turns)) * way
            dx = jnp.where(turn == 0, a, jnp.where(turn == 1, b, c))
            dy = jnp.where(turn == 0, b, jnp.where(turn == 1, c, a))
            dz = jnp.where(turn == 0, c, jnp.where(turn == 1, a, b))
            body(*neighbour(dx * sign + 4, dy * sign + 4, dz * sign + 4, core))
            return carry

        lax.fori_loop(0, 2 * size, step, 0)
    body(*neighbour(0, 0, 0, 1))


def sine(m):
    u = m.astype(F32) * (1.0 / 64.0)
    v = u * u
    p = 1.5148419e-4 * v - 4.673767e-3
    p = p * v + 7.968967e-2
    p = p * v - 6.4596371e-1
    p = p * v + 1.5707963
    return p * u * (1.0 / math.sqrt(NS))


def weights(phase):
    wcos = sine(jnp.abs((phase & 255) - 128) - 64)
    wsin = sine(jnp.abs(((phase - 64) & 255) - 128) - 64)
    return wcos.astype(BF16), wsin.astype(BF16)


def channel_kernel(
    raw, table, proto, steer, x_ref, power,
    rawb, tab, fb, turn, send, xv, xf, beam, wts, words, owns, packs, pack,
    raw_sem, tab_sem, send_sem, recv_sem, own_sem, x_sem, st_send, st_recv,
):
    inp, grp = lax.axis_index("inp"), lax.axis_index("grp")
    me = inp * N_GRP + grp

    x, ylo, z = inp // 8, inp // 4 % 2, inp % 4
    core = grp % 2
    mine = pl.ds(pl.multiple_of(core * 8, 8), 8)
    cuts = (0, 35, 67, 99, 131)

    def raw_copy(half, part):
        lo, hi = cuts[part] * NFFT, cuts[part + 1] * NFFT
        return pltpu.make_async_copy(
            raw.at[pl.ds(half * 16, 16), pl.ds(lo, hi - lo)],
            rawb.at[:, pl.ds(lo, hi - lo)], raw_sem.at[part])

    for part in range(4):
        raw_copy(0, part).start()
    tab_copy = pltpu.make_async_copy(table, tab, tab_sem)
    tab_copy.start()

    for_peers(lambda i, g: pl.semaphore_signal(
        pltpu.get_barrier_semaphore(), inc=1, device_id=(i, g), device_id_type=MESH))

    def pack_steer():
        low, high = steer[:, 0:128] & 255, steer[:, 128:256] & 255
        words[...] = jnp.zeros_like(words)
        words[0:NS_DEV, :] = (
            low + (pltpu.roll(low, 64, 1) << 8) + (high << 16) + (pltpu.roll(high, 64, 1) << 24))
        words[...] = words[...].T
        lane = lax.broadcasted_iota(jnp.int32, (4, 128), 1) // 8
        for chunk in range(CHUNKS):
            total = jnp.zeros((4, 128), jnp.int32)
            for eq in range(16):
                moved = pltpu.roll(words[eq * 4:(eq + 1) * 4, :], (eq - chunk) * 8 % 128, 1)
                total = jnp.where(lane == eq, moved, total)
            owns[chunk * 4:(chunk + 1) * 4, :] = total
        packs[x, ylo, z, grp, mine, :] = owns[mine, :]

    def filter_part(chunk, part):
        row = chunk % 2 * NS_CHUNK

        def body(it, carry):
            f0 = part * 32 + it // 8 * 16
            for sub in range(2):
                n0 = pl.multiple_of(it % 8 * 256 + sub * 128, 128)
                vals = [
                    rawb[:, pl.ds(pl.multiple_of((f0 + g) * NFFT + n0, 128), 128)]
                    .astype(F32)[row:row + NS_CHUNK]
                    for g in range(16 + TAPS - 1)
                ]
                taps = [proto[t:t + 1, pl.ds(n0, 128)] for t in range(TAPS)]
                for f in range(16):
                    acc = taps[0] * vals[f]
                    for t in range(1, TAPS):
                        acc = acc + taps[t] * vals[f + t]
                    turn[sub, f * NS_CHUNK:(f + 1) * NS_CHUNK, :] = acc
                for s in range(NS_CHUNK):
                    rows = turn[sub, pl.ds(s, 16, stride=NS_CHUNK), :].astype(BF16)
                    fb[pl.ds(pl.multiple_of(s * FRAMES + f0, 16), 16), pl.ds(n0, 128)] = rows
            return carry

        lax.fori_loop(0, 16, body, 0)

    def transform(chunk):
        def body(pair, carry):
            cols = fb[pl.ds(pl.multiple_of(pair * 256, 256), 256), :]
            for kt in range(4):
                out = lax.dot_general(
                    tab[kt * 256:(kt + 1) * 256, :], cols,
                    (((1,), (1,)), ((), ())), preferred_element_type=F32)
                first = out[:, :128].reshape(32, PARTS, 128)
                second = out[:, 128:].reshape(32, PARTS, 128)
                both = jnp.concatenate([first, second], axis=1).astype(BF16)
                send[chunk, kt * 32:(kt + 1) * 32, pl.ds(pl.multiple_of(pair * 16, 16), 16), :] = both
            return carry

        lax.fori_loop(0, NS_CHUNK // 2, body, 0)

    def own_copy(chunk):
        return pltpu.make_async_copy(
            send.at[chunk, me], xv.at[me, pl.ds(chunk * BLOCK, BLOCK)], own_sem.at[chunk])

    def spread(chunk):
        def one(i, g):
            pltpu.make_async_remote_copy(
                src_ref=send.at[chunk, i * N_GRP + g],
                dst_ref=xv.at[me, pl.ds(chunk * BLOCK, BLOCK)],
                send_sem=send_sem.at[chunk], recv_sem=recv_sem.at[chunk],
                device_id=(i, g), device_id_type=MESH).start()

        for_peers(one)
        own_copy(chunk).start()

    chip = pl.ds(grp // 2 * 2, 2)
    every = pl.ds(0, 4)
    near = pl.ds(0, 2)

    def steer_send(stage, src, offsets, dst=None):
        for off in offsets:
            pltpu.make_async_remote_copy(
                src_ref=src, dst_ref=src if dst is None else dst, send_sem=st_send.at[stage], recv_sem=st_recv.at[stage],
                device_id=neighbour(*off), device_id_type=MESH).start()

    along = [[tuple(k if axis == d else 0 for d in range(4)) for k in (1, 2, 3)] for axis in range(3)]

    def steer_start(stage):
        if stage == 0:
            other = pl.ds(pl.multiple_of((1 - core) * 8, 8), 8)
            steer_send(0, owns.at[other], [(0, 0, 0, 1)], packs.at[x, ylo, z, grp, other])
        elif stage == 4:
            steer_send(4, packs.at[every, near, every, every, mine], [(0, 0, 0, 1)])
        else:
            first = (packs.at[x, ylo, z, chip, mine], packs.at[x, near, z, every, mine],
                     packs.at[x, near, every, every, mine])[stage - 1]
            second = (packs.at[x, ylo, z, chip, mine], packs.at[every, ylo, z, chip, mine],
                      packs.at[every, near, z, every, mine])[stage - 1]

            @pl.when(core == 0)
            def _():
                steer_send(stage, first, along[(1, 2, 0)[stage - 1]])

            @pl.when(core == 1)
            def _():
                steer_send(stage, second, along[stage - 1])

    def steer_wait(stage):
        span = (
            packs.at[0, 0, 0, 0, mine], packs.at[0, 0, 0, pl.ds(0, 3)],
            packs.at[0, near, pl.ds(0, 3), every, mine],
            packs.at[pl.ds(0, 3), near, every, every, mine],
            packs.at[every, near, every, every, mine])[stage]
        done = pltpu.make_async_remote_copy(
            src_ref=span, dst_ref=span, send_sem=st_send.at[stage], recv_sem=st_recv.at[stage],
            device_id=neighbour(0, 0, 0, 1), device_id_type=MESH)
        done.wait_send()
        done.wait_recv()

    pack_steer()
    for chunk in range(CHUNKS):
        for part in range(4):
            if chunk % 2 == 0:
                raw_copy(chunk // 2, part).wait()
            filter_part(chunk, part)
            if chunk == 0:
                if part == 1:
                    pl.semaphore_wait(pltpu.get_barrier_semaphore(), COUNT - 1)
                elif part > 1:
                    steer_wait(part - 2)
                if part > 0:
                    steer_start(part - 1)
        if chunk == 1:
            for part in range(4):
                raw_copy(1, part).start()
        if chunk == 0:
            tab_copy.wait()
        transform(chunk)
        if chunk == 0:
            steer_wait(2)
            steer_start(3)
        spread(chunk)
        if chunk == 1:
            steer_wait(3)
            steer_start(4)
    steer_wait(4)

    lane = lax.broadcasted_iota(jnp.int32, (8, 128), 1) // 8

    def weigh(it, carry):
        two, tile = it // 8, it % 8
        for eq in range(16):
            total = jnp.zeros((8, 128), jnp.int32)
            for dd in range(16):
                block = packs[tile // 2, tile % 2, dd // 4, dd % 4, pl.ds(pl.multiple_of(two * 8, 8), 8), :]
                total = jnp.where(lane == dd, pltpu.roll(block, (dd - eq) * 8 % 128, 1), total)
            pack[0, eq * 4:(eq + 1) * 4, :] = total[0:4]
            pack[1, eq * 4:(eq + 1) * 4, :] = total[4:8]
        col = pl.multiple_of(tile * 128, 128)
        for one in range(2):
            for byte in range(4):
                index = (pack[one] >> (8 * byte)) & 255
                rows = slice(byte * 64, (byte + 1) * 64)
                for j in range(CH_DEV):
                    chan = inp * CH_DEV + ((NFFT // 2 // N_GRP - CH_GRP) // 2 + j)
                    wcos, wsin = weights(index * chan)
                    wts[j, two * 2 + one, rows, pl.ds(col, 128)] = wcos
                    wts[j, two * 2 + one, rows, pl.ds(col + KEYS, 128)] = wsin
        return carry

    lax.fori_loop(0, 16, weigh, 0)
    beam[...] = jnp.zeros_like(beam)

    def keep(chunk):
        rows = pl.ds(chunk * BLOCK, BLOCK)
        return pltpu.make_async_copy(xv.at[:, rows], x_ref.at[:, rows], x_sem.at[chunk])

    for chunk in range(CHUNKS):
        done = pltpu.make_async_remote_copy(
            src_ref=send.at[chunk, pl.ds(0, COUNT - 1)],
            dst_ref=xv.at[pl.ds(0, COUNT - 1), pl.ds(chunk * BLOCK, BLOCK)],
            send_sem=send_sem.at[chunk], recv_sem=recv_sem.at[chunk],
            device_id=(inp, (grp + 1) % 4), device_id_type=MESH)
        done.wait_send()
        done.wait_recv()
        own_copy(chunk).wait()
        keep(chunk).start()

        def add(sb, carry, chunk=chunk):
            block = xv[pl.ds(sb * 32, 32), chunk * BLOCK:(chunk + 1) * BLOCK, :]
            xf[...] = block.astype(F32).reshape(32 * BLOCK, 128)
            for j in range(CH_DEV):
                re = xf[pl.ds(2 * j, 256, stride=PARTS), :]
                im = xf[pl.ds(2 * j + 1, 256, stride=PARTS), :]
                ab = jnp.concatenate([re, im], axis=1).astype(BF16)
                ba = jnp.concatenate([im, -re], axis=1).astype(BF16)
                col = pl.multiple_of(sb * 256, 256)
                beam[j] += jnp.dot(
                    wts[j, chunk, :, pl.ds(col, 256)], ab, preferred_element_type=F32
                ) + jnp.dot(
                    wts[j, chunk, :, pl.ds(col + KEYS, 256)], ba, preferred_element_type=F32)
            return carry

        lax.fori_loop(0, KEYS // 256, add, 0)

    for j in range(CH_DEV):
        value = beam[j]
        square = value * value
        folded = (square[:, :128] + square[:, 128:]).T
        power[j:j + 1, :] = jnp.sum(folded, axis=0, keepdims=True) * (1.0 / FRAMES)
    for chunk in range(CHUNKS):
        keep(chunk).wait()


def gram_kernel(slots, x_ref, power_in, out, power, xb, xf, yfa, yfb, left, sems):
    step = pl.program_id(0)

    def gather(yf, first, count):
        for q in range(count):
            row = pl.multiple_of(slots[first + q] * PARTS, PARTS)
            yf[q * PARTS:(q + 1) * PARTS, :] = xf[pl.ds(row, PARTS), :]

    def pair(yf, j, count):
        return (yf[pl.ds(2 * j, count, stride=PARTS), :],
                yf[pl.ds(2 * j + 1, count, stride=PARTS), :])

    @pl.when(step == 0)
    def _():
        power[...] = power_in[...]
        copies = [
            pltpu.make_async_copy(
                x_ref.at[pl.ds(k * 16, 16)], xb.at[pl.ds(k * 16, 16)], sems.at[k]) for k in range(8)
        ]
        for copy in copies:
            copy.start()
        for k, copy in enumerate(copies):
            copy.wait()

            def widen(i, carry):
                dev = k * 16 + i
                rows = pl.ds(pl.multiple_of(dev * 256, 256), 256)
                xf[rows, :] = xb[dev].astype(F32)
                return carry

            lax.fori_loop(0, 16, widen, 0)
        gather(yfa, 0, 256)
        for j in range(CH_DEV):
            re, im = pair(yfa, j, ROWS)
            upper = jnp.concatenate([re, im], axis=1)
            lower = jnp.concatenate([-im, re], axis=1)
            left[j] = jnp.concatenate([upper, lower], axis=0).astype(BF16)

    def multiply(yf, col):
        for j in range(CH_DEV):
            right = jnp.concatenate(pair(yf, j, 256), axis=1).astype(BF16)
            prod = lax.dot_general(
                left[j], right, (((1,), (1,)), ((), ())), preferred_element_type=F32)
            prod = prod * (1.0 / FRAMES)
            out[0, j * ROWS:(j + 1) * ROWS, col:col + 256] = prod[:ROWS]
            out[1, j * ROWS:(j + 1) * ROWS, col:col + 256] = prod[ROWS:]

    gather(yfb, step * 512 + 256, 256)
    multiply(yfa, 0)
    gather(yfa, (step + 1) % (NS // 512) * 512, 256)
    multiply(yfb, 256)


def per_device(raw, steer, slot_map):
    anywhere = pl.BlockSpec(memory_space=pl.ANY)
    vmem = pl.BlockSpec(memory_space=pltpu.VMEM)
    dma = pltpu.SemaphoreType.DMA
    spectra, power = pl.pallas_call(
        channel_kernel,
        out_shape=(
            jax.ShapeDtypeStruct((COUNT, CHUNKS * BLOCK, FRAMES), BF16),
            jax.ShapeDtypeStruct((CH_DEV, BEAMS), F32),
        ),
        in_specs=[anywhere, anywhere, vmem, vmem],
        out_specs=(anywhere, vmem),
        scratch_shapes=[
            pltpu.VMEM((16, SAMPLES), BF16),
            pltpu.VMEM((COUNT * PARTS, NFFT), BF16),
            pltpu.VMEM((NS_CHUNK * FRAMES, NFFT), BF16),
            pltpu.VMEM((2, 16 * NS_CHUNK, 128), F32),
            pltpu.VMEM((CHUNKS, COUNT, BLOCK, FRAMES), BF16),
            pltpu.VMEM((COUNT, CHUNKS * BLOCK, FRAMES), BF16),
            pltpu.VMEM((32 * BLOCK, FRAMES), F32),
            pltpu.VMEM((CH_DEV, BEAMS, 2 * FRAMES), F32),
            pltpu.VMEM((CH_DEV, CHUNKS, BEAMS, 2 * KEYS), BF16),
            pltpu.VMEM((128, 128), jnp.int32),
            pltpu.VMEM((16, 128), jnp.int32),
            pltpu.VMEM((4, 2, 4, N_GRP, 16, 128), jnp.int32),
            pltpu.VMEM((2, 64, 128), jnp.int32),
            dma((4,)), dma, dma((CHUNKS,)), dma((CHUNKS,)), dma((CHUNKS,)), dma((CHUNKS,)),
            dma((5,)), dma((5,)),
        ],
        compiler_params=pltpu.CompilerParams(
            collective_id=0, has_side_effects=True, vmem_limit_bytes=62 * MIB),
        name="channelize",
    )(raw, jnp.asarray(dft_table()), jnp.asarray(prototype()), steer.T)
    visibility, power = pl.pallas_call(
        gram_kernel,
        out_shape=(
            jax.ShapeDtypeStruct((2, CH_DEV * ROWS, NS), F32),
            jax.ShapeDtypeStruct((CH_DEV, BEAMS), F32),
        ),
        grid=(NS // 512,),
        in_specs=[pl.BlockSpec(memory_space=pltpu.SMEM), anywhere, vmem],
        out_specs=(pl.BlockSpec((2, CH_DEV * ROWS, 512), lambda i: (0, 0, i)), vmem),
        scratch_shapes=[
            pltpu.VMEM((COUNT, CHUNKS * BLOCK, FRAMES), BF16),
            pltpu.VMEM((NS * PARTS, FRAMES), F32),
            pltpu.VMEM((256 * PARTS, FRAMES), F32),
            pltpu.VMEM((256 * PARTS, FRAMES), F32),
            pltpu.VMEM((CH_DEV, 2 * ROWS, 2 * FRAMES), BF16),
            dma((8,)),
        ],
        compiler_params=pltpu.CompilerParams(vmem_limit_bytes=48 * MIB),
        name="gram",
    )(slot_map, spectra, power)
    return visibility, power


def solution(mesh):
    in_specs = (P(("inp", "grp"), None), P(None, ("inp", "grp")), P())
    out_specs = (P(None, ("inp", "grp"), None), P(("inp", "grp"), None))
    return jax.shard_map(
        per_device, mesh=mesh, in_specs=in_specs, out_specs=out_specs, check_vma=False
    )
```

```python
import functools
import math

import jax
import jax.numpy as jnp
import numpy as np
from jax import lax
from jax.experimental import pallas as pl
from jax.experimental.pallas import tpu as pltpu
from jax.sharding import PartitionSpec as P

MESH = pl.DeviceIdType.MESH
NS = 4096
NFFT = 2048
BEAMS = 256
TAPS = 4
CH_GRP = 128
ROWS = 64
FRAMES = 128
N_INP = 32
N_GRP = 4
COUNT = N_INP * N_GRP
CH_DEV = CH_GRP * N_GRP // COUNT
NS_DEV = NS // COUNT
SAMPLES = (FRAMES + TAPS - 1) * NFFT
CHUNKS = 4
NS_CHUNK = NS_DEV // CHUNKS
PARTS = 2 * CH_DEV
BLOCK = NS_CHUNK * PARTS
KEYS = COUNT * NS_CHUNK
MIB = 2**20
F32 = jnp.float32
BF16 = jnp.bfloat16


def prototype():
    pos = np.arange(TAPS * NFFT, dtype=np.float64) + 0.5
    arg = pos / NFFT - TAPS / 2.0
    window = 0.5 - 0.5 * np.cos(2.0 * math.pi * pos / (TAPS * NFFT))
    return (np.sinc(arg) * window).reshape(TAPS, NFFT).astype(np.float32)


def dft_table():
    sub = NFFT // 2 // N_GRP
    order = np.arange(CH_GRP * N_GRP)
    device, inner = order // CH_DEV, order % CH_DEV
    chans = device % N_GRP * sub + (sub - CH_GRP) // 2 + device // N_GRP * CH_DEV + inner
    angle = 2.0 * math.pi * (chans[:, None] * np.arange(NFFT)[None, :] % NFFT) / NFFT
    both = np.stack([np.cos(angle), -np.sin(angle)], axis=1) / math.sqrt(NFFT)
    return both.astype(np.float32).astype(jnp.bfloat16).reshape(COUNT * PARTS, NFFT)


def orbits():
    seen, out = set(), []
    for a in range(4):
        for b in range(4):
            for c in range(4):
                if (a, b, c) == (0, 0, 0) or (a, b, c) in seen:
                    continue
                orbit = []
                for sign in (1, -1):
                    for turn in ((a, b, c), (b, c, a), (c, a, b)):
                        item = tuple(sign * v % 4 for v in turn)
                        if item not in orbit:
                            orbit.append(item)
                seen.update(orbit)
                out.append(orbit)
    return out


def neighbour(dx, dy, dz, dc):
    inp, grp = lax.axis_index("inp"), lax.axis_index("grp")
    x = (inp // 8 + dx) % 4
    y = (grp // 2 * 2 + inp // 4 % 2 + dy) % 4
    z = (inp % 4 + dz) % 4
    core = (grp % 2 + dc) % 2
    return x * 8 + y % 2 * 4 + z, y // 2 * 2 + core


def for_peers(body):
    way = 1 - 2 * (lax.axis_index("grp") % 2)
    for orbit in orbits():
        a, b, c = orbit[0]
        size = len(orbit)
        turns = 3 if size % 3 == 0 else 1

        def step(i, carry, a=a, b=b, c=c, size=size, turns=turns):
            core, item = i // size, i % size
            turn, sign = item % turns, (1 - 2 * (item // turns)) * way
            dx = jnp.where(turn == 0, a, jnp.where(turn == 1, b, c))
            dy = jnp.where(turn == 0, b, jnp.where(turn == 1, c, a))
            dz = jnp.where(turn == 0, c, jnp.where(turn == 1, a, b))
            body(*neighbour(dx * sign + 4, dy * sign + 4, dz * sign + 4, core))
            return carry

        lax.fori_loop(0, 2 * size, step, 0)
    body(*neighbour(0, 0, 0, 1))


def sine(m):
    u = m.astype(F32) * (1.0 / 64.0)
    v = u * u
    p = 1.5148419e-4 * v - 4.673767e-3
    p = p * v + 7.968967e-2
    p = p * v - 6.4596371e-1
    p = p * v + 1.5707963
    return p * u * (1.0 / math.sqrt(NS))


def weights(phase):
    wcos = sine(jnp.abs((phase & 255) - 128) - 64)
    wsin = sine(jnp.abs(((phase - 64) & 255) - 128) - 64)
    return wcos.astype(BF16), wsin.astype(BF16)


def channel_kernel(
    raw, table, proto, steer, x_ref, power,
    rawb, tab, fb, turn, send, xv, xf, beam, wts, words, owns, packs, pack,
    raw_sem, tab_sem, send_sem, recv_sem, own_sem, x_sem, st_send, st_recv,
):
    inp, grp = lax.axis_index("inp"), lax.axis_index("grp")
    me = inp * N_GRP + grp

    x, ylo, z = inp // 8, inp // 4 % 2, inp % 4
    core = grp % 2
    mine = pl.ds(pl.multiple_of(core * 8, 8), 8)
    cuts = (0, 35, 67, 99, 131)

    def raw_copy(half, part):
        lo, hi = cuts[part] * NFFT, cuts[part + 1] * NFFT
        return pltpu.make_async_copy(
            raw.at[pl.ds(half * 16, 16), pl.ds(lo, hi - lo)],
            rawb.at[:, pl.ds(lo, hi - lo)], raw_sem.at[part])

    for part in range(4):
        raw_copy(0, part).start()
    tab_copy = pltpu.make_async_copy(table, tab, tab_sem)
    tab_copy.start()

    for_peers(lambda i, g: pl.semaphore_signal(
        pltpu.get_barrier_semaphore(), inc=1, device_id=(i, g), device_id_type=MESH))

    def pack_steer():
        low, high = steer[:, 0:128] & 255, steer[:, 128:256] & 255
        words[...] = jnp.zeros_like(words)
        words[0:NS_DEV, :] = (
            low + (pltpu.roll(low, 64, 1) << 8) + (high << 16) + (pltpu.roll(high, 64, 1) << 24))
        words[...] = words[...].T
        lane = lax.broadcasted_iota(jnp.int32, (4, 128), 1) // 8
        for chunk in range(CHUNKS):
            total = jnp.zeros((4, 128), jnp.int32)
            for eq in range(16):
                moved = pltpu.roll(words[eq * 4:(eq + 1) * 4, :], (eq - chunk) * 8 % 128, 1)
                total = jnp.where(lane == eq, moved, total)
            owns[chunk * 4:(chunk + 1) * 4, :] = total
        packs[x, ylo, z, grp, mine, :] = owns[mine, :]

    def filter_part(chunk, part):
        row = chunk % 2 * NS_CHUNK

        def body(it, carry):
            f0 = part * 32 + it // 8 * 16
            for sub in range(2):
                n0 = pl.multiple_of(it % 8 * 256 + sub * 128, 128)
                vals = [
                    rawb[:, pl.ds(pl.multiple_of((f0 + g) * NFFT + n0, 128), 128)]
                    .astype(F32)[row:row + NS_CHUNK]
                    for g in range(16 + TAPS - 1)
                ]
                taps = [proto[t:t + 1, pl.ds(n0, 128)] for t in range(TAPS)]
                for f in range(16):
                    acc = taps[0] * vals[f]
                    for t in range(1, TAPS):
                        acc = acc + taps[t] * vals[f + t]
                    turn[sub, f * NS_CHUNK:(f + 1) * NS_CHUNK, :] = acc
                for s in range(NS_CHUNK):
                    rows = turn[sub, pl.ds(s, 16, stride=NS_CHUNK), :].astype(BF16)
                    fb[pl.ds(pl.multiple_of(s * FRAMES + f0, 16), 16), pl.ds(n0, 128)] = rows
            return carry

        lax.fori_loop(0, 16, body, 0)

    def transform(chunk, begin, end):
        def body(pair, carry):
            cols = fb[pl.ds(pl.multiple_of(pair * 256, 256), 256), :]
            for kt in range(4):
                out = lax.dot_general(
                    tab[kt * 256:(kt + 1) * 256, :], cols,
                    (((1,), (1,)), ((), ())), preferred_element_type=F32)
                first = out[:, :128].reshape(32, PARTS, 128)
                second = out[:, 128:].reshape(32, PARTS, 128)
                both = jnp.concatenate([first, second], axis=1).astype(BF16)
                send[chunk, kt * 32:(kt + 1) * 32, pl.ds(pl.multiple_of(pair * 16, 16), 16), :] = both
            return carry

        lax.fori_loop(begin, end, body, 0)

    def own_copy(chunk):
        return pltpu.make_async_copy(
            send.at[chunk, me], xv.at[me, pl.ds(chunk * BLOCK, BLOCK)], own_sem.at[chunk])

    def spread(chunk, begin, end):
        rows = (end - begin) * 2 * PARTS

        def one(i, g):
            pltpu.make_async_remote_copy(
                src_ref=send.at[chunk, i * N_GRP + g, pl.ds(begin * 2 * PARTS, rows)],
                dst_ref=xv.at[me, pl.ds(chunk * BLOCK + begin * 2 * PARTS, rows)],
                send_sem=send_sem.at[chunk], recv_sem=recv_sem.at[chunk],
                device_id=(i, g), device_id_type=MESH).start()

        for_peers(one)

    chip = pl.ds(grp // 2 * 2, 2)
    every = pl.ds(0, 4)
    near = pl.ds(0, 2)

    def steer_send(stage, src, offsets, dst=None):
        for off in offsets:
            pltpu.make_async_remote_copy(
                src_ref=src, dst_ref=src if dst is None else dst, send_sem=st_send.at[stage], recv_sem=st_recv.at[stage],
                device_id=neighbour(*off), device_id_type=MESH).start()

    along = [[tuple(k if axis == d else 0 for d in range(4)) for k in (1, 2, 3)] for axis in range(3)]

    def steer_start(stage):
        if stage == 0:
            other = pl.ds(pl.multiple_of((1 - core) * 8, 8), 8)
            steer_send(0, owns.at[other], [(0, 0, 0, 1)], packs.at[x, ylo, z, grp, other])
        elif stage == 4:
            steer_send(4, packs.at[every, near, every, every, mine], [(0, 0, 0, 1)])
        else:
            first = (packs.at[x, ylo, z, chip, mine], packs.at[x, near, z, every, mine],
                     packs.at[x, near, every, every, mine])[stage - 1]
            second = (packs.at[x, ylo, z, chip, mine], packs.at[every, ylo, z, chip, mine],
                      packs.at[every, near, z, every, mine])[stage - 1]

            @pl.when(core == 0)
            def _():
                steer_send(stage, first, along[(1, 2, 0)[stage - 1]])

            @pl.when(core == 1)
            def _():
                steer_send(stage, second, along[stage - 1])

    def steer_wait(stage):
        span = (
            packs.at[0, 0, 0, 0, mine], packs.at[0, 0, 0, pl.ds(0, 3)],
            packs.at[0, near, pl.ds(0, 3), every, mine],
            packs.at[pl.ds(0, 3), near, every, every, mine],
            packs.at[every, near, every, every, mine])[stage]
        done = pltpu.make_async_remote_copy(
            src_ref=span, dst_ref=span, send_sem=st_send.at[stage], recv_sem=st_recv.at[stage],
            device_id=neighbour(0, 0, 0, 1), device_id_type=MESH)
        done.wait_send()
        done.wait_recv()

    pack_steer()
    for chunk in range(CHUNKS):
        for part in range(4):
            if chunk % 2 == 0:
                raw_copy(chunk // 2, part).wait()
            filter_part(chunk, part)
            if chunk == 0:
                if part == 1:
                    pl.semaphore_wait(pltpu.get_barrier_semaphore(), COUNT - 1)
                elif part > 1:
                    steer_wait(part - 2)
                if part > 0:
                    steer_start(part - 1)
        if chunk == 1:
            for part in range(4):
                raw_copy(1, part).start()
        if chunk == 0:
            tab_copy.wait()
            transform(chunk, 0, 2)
            steer_wait(2)
            steer_start(3)
            spread(chunk, 0, 2)
            transform(chunk, 2, 4)
            spread(chunk, 2, 4)
        else:
            transform(chunk, 0, 4)
            spread(chunk, 0, 4)
        own_copy(chunk).start()
        if chunk == 1:
            steer_wait(3)
            steer_start(4)
    steer_wait(4)

    lane = lax.broadcasted_iota(jnp.int32, (8, 128), 1) // 8

    def weigh(it, carry):
        two, tile = it // 8, it % 8
        for eq in range(16):
            total = jnp.zeros((8, 128), jnp.int32)
            for dd in range(16):
                block = packs[tile // 2, tile % 2, dd // 4, dd % 4, pl.ds(pl.multiple_of(two * 8, 8), 8), :]
                total = jnp.where(lane == dd, pltpu.roll(block, (dd - eq) * 8 % 128, 1), total)
            pack[0, eq * 4:(eq + 1) * 4, :] = total[0:4]
            pack[1, eq * 4:(eq + 1) * 4, :] = total[4:8]
        col = pl.multiple_of(tile * 128, 128)
        for one in range(2):
            for byte in range(4):
                index = (pack[one] >> (8 * byte)) & 255
                rows = slice(byte * 64, (byte + 1) * 64)
                for j in range(CH_DEV):
                    chan = inp * CH_DEV + ((NFFT // 2 // N_GRP - CH_GRP) // 2 + j)
                    wcos, wsin = weights(index * chan)
                    wts[j, two * 2 + one, rows, pl.ds(col, 128)] = wcos
                    wts[j, two * 2 + one, rows, pl.ds(col + KEYS, 128)] = wsin
        return carry

    lax.fori_loop(0, 16, weigh, 0)
    beam[...] = jnp.zeros_like(beam)

    def keep(chunk):
        rows = pl.ds(chunk * BLOCK, BLOCK)
        return pltpu.make_async_copy(xv.at[:, rows], x_ref.at[:, rows], x_sem.at[chunk])

    for chunk in range(CHUNKS):
        done = pltpu.make_async_remote_copy(
            src_ref=send.at[chunk, pl.ds(0, COUNT - 1)],
            dst_ref=xv.at[pl.ds(0, COUNT - 1), pl.ds(chunk * BLOCK, BLOCK)],
            send_sem=send_sem.at[chunk], recv_sem=recv_sem.at[chunk],
            device_id=(inp, (grp + 1) % 4), device_id_type=MESH)
        done.wait_send()
        done.wait_recv()
        own_copy(chunk).wait()
        keep(chunk).start()

        def add(sb, carry, chunk=chunk):
            block = xv[pl.ds(sb * 32, 32), chunk * BLOCK:(chunk + 1) * BLOCK, :]
            xf[...] = block.astype(F32).reshape(32 * BLOCK, 128)
            for j in range(CH_DEV):
                re = xf[pl.ds(2 * j, 256, stride=PARTS), :]
                im = xf[pl.ds(2 * j + 1, 256, stride=PARTS), :]
                ab = jnp.concatenate([re, im], axis=1).astype(BF16)
                ba = jnp.concatenate([im, -re], axis=1).astype(BF16)
                col = pl.multiple_of(sb * 256, 256)
                beam[j] += jnp.dot(
                    wts[j, chunk, :, pl.ds(col, 256)], ab, preferred_element_type=F32
                ) + jnp.dot(
                    wts[j, chunk, :, pl.ds(col + KEYS, 256)], ba, preferred_element_type=F32)
            return carry

        lax.fori_loop(0, KEYS // 256, add, 0)

    for j in range(CH_DEV):
        value = beam[j]
        square = value * value
        folded = (square[:, :128] + square[:, 128:]).T
        power[j:j + 1, :] = jnp.sum(folded, axis=0, keepdims=True) * (1.0 / FRAMES)
    for chunk in range(CHUNKS):
        keep(chunk).wait()


def gram_kernel(slots, x_ref, power_in, out, power, xb, xf, yfa, yfb, left, sems):
    step = pl.program_id(0)

    def gather(yf, first, count):
        for q in range(count):
            row = pl.multiple_of(slots[first + q] * PARTS, PARTS)
            yf[q * PARTS:(q + 1) * PARTS, :] = xf[pl.ds(row, PARTS), :]

    def pair(yf, j, count):
        return (yf[pl.ds(2 * j, count, stride=PARTS), :],
                yf[pl.ds(2 * j + 1, count, stride=PARTS), :])

    @pl.when(step == 0)
    def _():
        power[...] = power_in[...]
        copies = [
            pltpu.make_async_copy(
                x_ref.at[pl.ds(k * 16, 16)], xb.at[pl.ds(k * 16, 16)], sems.at[k]) for k in range(8)
        ]
        for copy in copies:
            copy.start()
        for k, copy in enumerate(copies):
            copy.wait()

            def widen(i, carry):
                dev = k * 16 + i
                rows = pl.ds(pl.multiple_of(dev * 256, 256), 256)
                xf[rows, :] = xb[dev].astype(F32)
                return carry

            lax.fori_loop(0, 16, widen, 0)
        gather(yfa, 0, 256)
        for j in range(CH_DEV):
            re, im = pair(yfa, j, ROWS)
            upper = jnp.concatenate([re, im], axis=1)
            lower = jnp.concatenate([-im, re], axis=1)
            left[j] = jnp.concatenate([upper, lower], axis=0).astype(BF16)

    def multiply(yf, col):
        for j in range(CH_DEV):
            right = jnp.concatenate(pair(yf, j, 256), axis=1).astype(BF16)
            prod = lax.dot_general(
                left[j], right, (((1,), (1,)), ((), ())), preferred_element_type=F32)
            prod = prod * (1.0 / FRAMES)
            out[0, j * ROWS:(j + 1) * ROWS, col:col + 256] = prod[:ROWS]
            out[1, j * ROWS:(j + 1) * ROWS, col:col + 256] = prod[ROWS:]

    gather(yfb, step * 512 + 256, 256)
    multiply(yfa, 0)
    gather(yfa, (step + 1) % (NS // 512) * 512, 256)
    multiply(yfb, 256)


def per_device(raw, steer, slot_map):
    anywhere = pl.BlockSpec(memory_space=pl.ANY)
    vmem = pl.BlockSpec(memory_space=pltpu.VMEM)
    dma = pltpu.SemaphoreType.DMA
    spectra, power = pl.pallas_call(
        channel_kernel,
        out_shape=(
            jax.ShapeDtypeStruct((COUNT, CHUNKS * BLOCK, FRAMES), BF16),
            jax.ShapeDtypeStruct((CH_DEV, BEAMS), F32),
        ),
        in_specs=[anywhere, anywhere, vmem, vmem],
        out_specs=(anywhere, vmem),
        scratch_shapes=[
            pltpu.VMEM((16, SAMPLES), BF16),
            pltpu.VMEM((COUNT * PARTS, NFFT), BF16),
            pltpu.VMEM((NS_CHUNK * FRAMES, NFFT), BF16),
            pltpu.VMEM((2, 16 * NS_CHUNK, 128), F32),
            pltpu.VMEM((CHUNKS, COUNT, BLOCK, FRAMES), BF16),
            pltpu.VMEM((COUNT, CHUNKS * BLOCK, FRAMES), BF16),
            pltpu.VMEM((32 * BLOCK, FRAMES), F32),
            pltpu.VMEM((CH_DEV, BEAMS, 2 * FRAMES), F32),
            pltpu.VMEM((CH_DEV, CHUNKS, BEAMS, 2 * KEYS), BF16),
            pltpu.VMEM((128, 128), jnp.int32),
            pltpu.VMEM((16, 128), jnp.int32),
            pltpu.VMEM((4, 2, 4, N_GRP, 16, 128), jnp.int32),
            pltpu.VMEM((2, 64, 128), jnp.int32),
            dma((4,)), dma, dma((CHUNKS,)), dma((CHUNKS,)), dma((CHUNKS,)), dma((CHUNKS,)),
            dma((5,)), dma((5,)),
        ],
        compiler_params=pltpu.CompilerParams(
            collective_id=0, has_side_effects=True, vmem_limit_bytes=62 * MIB),
        name="channelize",
    )(raw, jnp.asarray(dft_table()), jnp.asarray(prototype()), steer.T)
    visibility, power = pl.pallas_call(
        gram_kernel,
        out_shape=(
            jax.ShapeDtypeStruct((2, CH_DEV * ROWS, NS), F32),
            jax.ShapeDtypeStruct((CH_DEV, BEAMS), F32),
        ),
        grid=(NS // 512,),
        in_specs=[pl.BlockSpec(memory_space=pltpu.SMEM), anywhere, vmem],
        out_specs=(pl.BlockSpec((2, CH_DEV * ROWS, 512), lambda i: (0, 0, i)), vmem),
        scratch_shapes=[
            pltpu.VMEM((COUNT, CHUNKS * BLOCK, FRAMES), BF16),
            pltpu.VMEM((NS * PARTS, FRAMES), F32),
            pltpu.VMEM((256 * PARTS, FRAMES), F32),
            pltpu.VMEM((256 * PARTS, FRAMES), F32),
            pltpu.VMEM((CH_DEV, 2 * ROWS, 2 * FRAMES), BF16),
            dma((8,)),
        ],
        compiler_params=pltpu.CompilerParams(vmem_limit_bytes=48 * MIB),
        name="gram",
    )(slot_map, spectra, power)
    return visibility, power


def solution(mesh):
    in_specs = (P(("inp", "grp"), None), P(None, ("inp", "grp")), P())
    out_specs = (P(None, ("inp", "grp"), None), P(("inp", "grp"), None))
    return jax.shard_map(
        per_device, mesh=mesh, in_specs=in_specs, out_specs=out_specs, check_vma=False
    )
```
